32 devices in a mesh: dp: 8 (over z, x), seq: 4 (over y, core).
Axes of the slice: x: 2, y: 2, z: 4, core: 2. Of those that a mesh axis runs over, the one named last changes fastest.
Arguments:
- hidden_in: bfloat16 [16384, 640], P(('dp', 'seq')), may hold values from -6 to 6
- cotangent: bfloat16 [16384, 640], P(('dp', 'seq')), may hold values from -6 to 6
- seg_ids: int32 [8, 2048], P('dp'), may hold values from 0 to 2, as said below
- positions: int32 [8, 2048], P('dp'), may hold values from 0 to 2559, as said below
- norm_gains: bfloat16 [3072], P(('dp', 'seq')), may hold values from 0.25 to 1.75
- w_qkv: bfloat16 [640, 1536], P(None, ('dp', 'seq')), may hold values from -0.25 to 0.25
- w_out: bfloat16 [1024, 640], P(('dp', 'seq')), may hold values from -0.1875 to 0.1875
- w_gate_up: bfloat16 [640, 4096], P(None, ('dp', 'seq')), may hold values from -0.25 to 0.25
- w_down: bfloat16 [2048, 640], P(('dp', 'seq')), may hold values from -0.125 to 0.125
Outputs:
- output: bfloat16 [16384, 640], P(('dp', 'seq'))
- input_grad: float32 [16384, 640], P(('dp', 'seq'))
- gain_grad: float32 [3072], P(('dp', 'seq'))
- qkv_grad: float32 [640, 1536], P(None, ('dp', 'seq'))
- out_proj_grad: float32 [1024, 640], P(('dp', 'seq'))
- gate_up_grad: float32 [640, 4096], P(None, ('dp', 'seq'))
- down_grad: float32 [2048, 640], P(('dp', 'seq'))
The draws below stay inside these ranges and needn't reach their ends.
Inputs may be any that keep to these rules, and one draw needn't show every extreme that they name: `seg_ids`: along a row of 2048 tokens the ids never fall, so each id covers consecutive tokens; one id covers tokens on every device of its group. `positions`: positions rise by one from each token to the next token with the same id; in every group the tokens of the first id end at position 2559.
All inputs are finite; a program needn't handle non-finite values.
Results may differ from the reference program's by a relative error of at most 0.015.
Values may be sent and summed in bfloat16 or wider, within the bound.
A program may use at most 128 MiB of HBM per device.

```python
import jax
import jax.numpy as jnp
from jax import lax

D = 640
H = 4
HD = 256
FF = 2048
WINDOW = 512
TOK_DEV = 512
GLEN = 2048
GROUPS = 8
TOKENS = 16384
GAINS = 3072


def doc_layout(key):
    head_key, tail_key = jax.random.split(key, 2)
    head_len = jax.random.randint(head_key, (GROUPS, 1), 1, TOK_DEV // 2 + 1)
    tail_len = jax.random.randint(tail_key, (GROUPS, 1), 1, TOK_DEV // 2 + 1)
    head_last = GLEN + WINDOW - 1
    slots = jnp.arange(GLEN, dtype=jnp.int32)[None, :]
    tail_start = GLEN - tail_len
    doc_ids = jnp.where(slots < head_len, 0, jnp.where(slots >= tail_start, 2, 1))
    doc_pos = jnp.where(slots < head_len, head_last - head_len + 1 + slots, jnp.where(slots >= tail_start, slots - tail_start, slots - head_len))
    return (doc_ids.astype(jnp.int32), doc_pos.astype(jnp.int32))


def draw_seg_ids(key, part):
    return doc_layout(key)[0]


def draw_positions(key, part):
    return doc_layout(key)[1]


def draw_cotangent(key, part):
    key = jax.random.fold_in(key, 11)
    ramp_pos = jnp.arange(TOKENS, dtype=jnp.float32) / (TOKENS - 1)
    base_val = jnp.clip(jax.random.normal(key, (TOKENS, D), jnp.float32), -4.0, 4.0)
    ramp_val = 0.5 + ramp_pos
    return jnp.clip(base_val * ramp_val[:, None], -6.0, 6.0).astype(jnp.bfloat16)


def block_scale(stream_key, dims, pieces, smallest, high):
    loudness = 1.0
    for dim, blocks in pieces:
        draws = jax.random.uniform(jax.random.fold_in(jax.random.fold_in(stream_key, 6), dim), (blocks,), jnp.float32, smallest / len(pieces), high / len(pieces))
        loudness = loudness * jnp.repeat(jnp.exp(draws), dims[dim] // blocks).reshape((-1,) + (1,) * (len(dims) - 1 - dim))
    return loudness


def noise(own_key, shape, width, bound, cuts=(), held_as=jnp.bfloat16):
    loudness = block_scale(own_key, shape, cuts, -0.22, 0.18) if cuts else 1.0
    entries = jax.random.normal(own_key, shape, jnp.float32) * width * loudness
    return jnp.minimum(jnp.maximum(entries, -bound), bound).astype(held_as)


def setup_inputs(seed: int = 0) -> dict:
    splits = jax.random.split(jax.random.key(seed), 10)
    return {
        "hidden_in": noise(splits[0], (TOKENS, D), 1.0, 6.0, ((0, 32),)),
        "cotangent": draw_cotangent(jax.random.fold_in(splits[9], 71), 0),
        "seg_ids": draw_seg_ids(jax.random.fold_in(splits[9], 71), 0),
        "positions": draw_positions(jax.random.fold_in(splits[9], 71), 0),
        "norm_gains": jnp.clip(1.0 + 0.15 * jax.random.normal(splits[4], (GAINS,), jnp.float32), 0.25, 1.75).astype(jnp.bfloat16),
        "w_qkv": noise(splits[5], (D, (H + 2) * HD), D ** -0.5, 0.25, ((1, 32),)),
        "w_out": noise(splits[6], (H * HD, D), (H * HD) ** -0.5, 0.1875, ((0, 32),)),
        "w_gate_up": noise(splits[7], (D, 2 * FF), D ** -0.5, 0.25, ((1, 32),)),
        "w_down": noise(splits[8], (FF, D), FF ** -0.5, 0.125, ((0, 32),)),
    }


@jax.custom_vjp
def low(v):
    return lax.optimization_barrier(v.astype(jnp.bfloat16)).astype(jnp.float32)

@jax.custom_vjp
def low_back(v):
    return v

def low_keep(v):
    return (low(v), None)

def low_pass(kept, grad):
    return (grad,)

def back_keep(v):
    return (v, None)

def back_low(kept, grad):
    return (low(grad),)
low.defvjp(low_keep, low_pass)
low_back.defvjp(back_keep, back_low)
NORM_EPS = 1e-06
MASKED_OUT = -1e+30
PRECISE = lax.Precision.HIGHEST

def mat_mul(left_arr, right_arr):
    return jnp.dot(left_arr, right_arr, precision=PRECISE)

def rms_scale(values, gain):
    return values * lax.rsqrt(lax.optimization_barrier(jnp.mean(values * values, -1, keepdims=True)) + NORM_EPS) * gain

def turn_angles(pos_vals):
    half_dim = HD // 2
    inverse_freq = jnp.power(10000.0, -(2.0 * jnp.arange(half_dim, dtype=jnp.float32)) / HD)
    return pos_vals.astype(jnp.float32)[:, None] * inverse_freq[None, :]

def rope_turn(values, angles):
    half_dim = values.shape[-1] // 2
    first_half = values[..., :half_dim]
    second_half = values[..., half_dim:]
    cosine = jnp.cos(angles)
    sine_val = jnp.sin(angles)
    return jnp.concatenate([first_half * cosine - second_half * sine_val, second_half * cosine + first_half * sine_val], -1)

def layer_forward(hidden, weight_set, pos_row, id_row):
    gain_vec, qkv_mat, out_mat, gate_up_mat, down_mat = weight_set
    gain_in = gain_vec[0:D]
    gain_attn_post = gain_vec[D:2 * D]
    gain_ffn_pre = gain_vec[2 * D:3 * D]
    gain_ffn_post = gain_vec[3 * D:4 * D]
    gain_query = gain_vec[4 * D:4 * D + HD]
    gain_key = gain_vec[4 * D + HD:4 * D + 2 * HD]
    attn_in = low(rms_scale(hidden, gain_in))
    projected = mat_mul(attn_in, qkv_mat)
    query_raw = low_back(projected[:, :H * HD]).reshape(-1, H, HD)
    key_raw = low_back(projected[:, H * HD:(H + 1) * HD])
    value_low = low(low_back(projected[:, (H + 1) * HD:]))
    angles = turn_angles(pos_row)
    query_low = low(rope_turn(rms_scale(query_raw, gain_query), angles[:, None, :]) * HD ** (-0.5))
    key_low = low(rope_turn(rms_scale(key_raw, gain_key), angles))
    scores = low_back(jnp.einsum('qhd,kd->hqk', query_low, key_low, precision=PRECISE))
    pos_gap = pos_row[:, None] - pos_row[None, :]
    allowed = (id_row[:, None] == id_row[None, :]) & (pos_gap >= 0) & (pos_gap < WINDOW)
    probs_low = low(jax.nn.softmax(jnp.where(allowed[None], scores, MASKED_OUT), axis=-1))
    attended = jnp.einsum('hqk,kd->qhd', probs_low, value_low, precision=PRECISE).reshape(-1, H * HD)
    attended = low(low_back(attended))
    branch = low_back(mat_mul(attended, out_mat))
    middle = hidden + rms_scale(branch, gain_attn_post)
    ffn_in = low(rms_scale(middle, gain_ffn_pre))
    gate_up = mat_mul(ffn_in, gate_up_mat)
    gate_val = low_back(gate_up[:, :FF])
    up_val = low_back(gate_up[:, FF:])
    mixed = low(jax.nn.gelu(gate_val, approximate=True) * up_val)
    down_val = low_back(mat_mul(mixed, down_mat))
    return middle + rms_scale(down_val, gain_ffn_post)

def reference(hidden_in, cotangent, seg_ids, positions, norm_gains, w_qkv, w_out, w_gate_up, w_down):
    weights = tuple((weight_arr.astype(jnp.float32) for weight_arr in (norm_gains, w_qkv, w_out, w_gate_up, w_down)))
    group_in = hidden_in.astype(jnp.float32).reshape(GROUPS, GLEN, D)
    group_cot = cotangent.astype(jnp.float32).reshape(GROUPS, GLEN, D)

    def one_group(totals, inputs):
        layer_in, layer_cot, pos_row, id_row = inputs

        def run_layer(hidden, weight_set):
            return layer_forward(hidden, weight_set, pos_row, id_row)
        layer_out, pull_back = jax.vjp(run_layer, layer_in, weights)
        grad_in, grad_weights = pull_back(layer_cot)
        totals = jax.tree.map(lambda left_val, right_val: left_val + right_val, totals, grad_weights)
        return (totals, (layer_out.astype(jnp.bfloat16), grad_in))
    zero_totals = jax.tree.map(jnp.zeros_like, weights)
    totals, (outputs, grad_rows) = lax.scan(one_group, zero_totals, (group_in, group_cot, positions, seg_ids))
    return (outputs.reshape(TOKENS, D), grad_rows.reshape(TOKENS, D), totals[0], totals[1], totals[2], totals[3], totals[4])
```

```python
import jax
import jax.numpy as jnp
from jax import lax
from jax.sharding import PartitionSpec as P

D = 640
H = 4
HD = 256
FF = 2048
WINDOW = 512


NORM_EPS = 1e-06
MASKED_OUT = -1e30


def from_behind(block, axis, distance):
    devices = range(lax.axis_size(axis))
    route = [(i - distance, i) for i in devices if i - distance in devices]
    return lax.ppermute(block, axis, route)


def norm_forward(values):
    inverse = lax.rsqrt(jnp.mean(values * values, -1, keepdims=True) + NORM_EPS)
    return (values * inverse, inverse)


def norm_back(normed, inverse, grad_normed):
    return inverse * (grad_normed - normed * jnp.mean(grad_normed * normed, -1, keepdims=True))


def turn_angles(pos_vals):
    half_dim = HD // 2
    inverse_freq = jnp.power(10000.0, -(2.0 * jnp.arange(half_dim, dtype=jnp.float32)) / HD)
    return pos_vals.astype(jnp.float32)[:, None] * inverse_freq[None, :]


def rope_turn(values, angles):
    half_dim = values.shape[-1] // 2
    first_half = values[..., :half_dim]
    second_half = values[..., half_dim:]
    cosine = jnp.cos(angles)
    sine_val = jnp.sin(angles)
    return jnp.concatenate(
        [
            first_half * cosine - second_half * sine_val,
            second_half * cosine + first_half * sine_val,
        ],
        -1,
    )


def rope_back(grads, angles):
    half_dim = grads.shape[-1] // 2
    first_half = grads[..., :half_dim]
    second_half = grads[..., half_dim:]
    cosine = jnp.cos(angles)
    sine_val = jnp.sin(angles)
    return jnp.concatenate(
        [
            first_half * cosine + second_half * sine_val,
            second_half * cosine - first_half * sine_val,
        ],
        -1,
    )


def split_gains(gain_vec):
    return (
        gain_vec[0:D],
        gain_vec[D : 2 * D],
        gain_vec[2 * D : 3 * D],
        gain_vec[3 * D : 4 * D],
        gain_vec[4 * D : 4 * D + HD],
        gain_vec[4 * D + HD : 4 * D + 2 * HD],
    )


def bit_orders():
    dp_bits = lax.axis_size("dp").bit_length() - 1
    seq_bits = lax.axis_size("seq").bit_length() - 1
    places = [("dp", b) for b in reversed(range(dp_bits))]
    places += [("seq", b) for b in reversed(range(seq_bits))]
    first = [("dp", b) for b in reversed(range(1, dp_bits))]
    low_dp = [("dp", 0)]
    high_seq = [("seq", b) for b in reversed(range(1, seq_bits))]
    last = [("seq", 0)]
    return places, first + low_dp + high_seq + last, first + high_seq + low_dp + last


def swap(block, axis, bit):
    route = [(i, i ^ (1 << bit)) for i in range(lax.axis_size(axis))]
    return lax.ppermute(block, axis, route)


def own_bit(axis, bit):
    return (lax.axis_index(axis) >> bit) & 1


def gather_rows(block, order, places):
    rows, columns = block.shape
    have = []
    for axis, bit in order:
        other = swap(block, axis, bit)
        at = sum(1 for h in have if places.index(h) < places.index((axis, bit)))
        upper = own_bit(axis, bit) == 1
        block = jnp.stack([jnp.where(upper, other, block), jnp.where(upper, block, other)], at)
        have.append((axis, bit))
    return block.reshape(-1, rows, columns)


def scatter_rows(blocks, order, places):
    rows, columns = blocks.shape[1:]
    block = blocks.reshape((2,) * len(places) + (rows, columns))
    left = list(places)
    for step, (axis, bit) in enumerate(reversed(order)):
        at = left.index((axis, bit))
        mine = own_bit(axis, bit)
        give = lax.dynamic_index_in_dim(block, 1 - mine, at, keepdims=False)
        keep = lax.dynamic_index_in_dim(block, mine, at, keepdims=False)
        got = swap(give, axis, bit)
        block = keep.astype(jnp.float32) + got.astype(jnp.float32)
        if step < len(order) - 1:
            block = block.astype(jnp.bfloat16)
        left.remove((axis, bit))
    return block


def scatter_exact(values, order, places):
    block = values.reshape((2,) * len(places) + (-1,))
    left = list(places)
    for axis, bit in reversed(order):
        at = left.index((axis, bit))
        mine = own_bit(axis, bit)
        give = lax.dynamic_index_in_dim(block, 1 - mine, at, keepdims=False)
        keep = lax.dynamic_index_in_dim(block, mine, at, keepdims=False)
        block = keep + swap(give, axis, bit)
        left.remove((axis, bit))
    return block


def body(hidden_in, cotangent, seg_ids, positions, norm_gains, w_qkv, w_out, w_gate_up, w_down):
    row_count = hidden_in.shape[0]
    seq_count = lax.axis_size("seq")
    seq_place = lax.axis_index("seq")
    reach_count = min(seq_count - 1, (WINDOW + row_count - 2) // row_count)
    query_scale = HD ** (-0.5)
    places, order_a, order_b = bit_orders()
    device_count = lax.axis_size("dp") * seq_count
    gain_len = norm_gains.shape[0]
    qkv_rows = w_qkv.shape[1]
    half_rows = w_down.shape[0]
    gain_row = jnp.pad(norm_gains.reshape(1, gain_len), ((0, 15), (0, D - gain_len)))
    first_pack = jnp.concatenate([w_qkv.T, gain_row], 0)
    first_full = gather_rows(first_pack, order_a, places)
    out_full = gather_rows(w_out, order_b, places).reshape(H * HD, D)
    up_t = w_gate_up.T
    gate_up_full = [
        gather_rows(up_t[:half_rows], order_a, places),
        gather_rows(up_t[half_rows:], order_b, places),
    ]
    down_all = gather_rows(w_down, order_a, places).reshape(-1, 2, half_rows, D)
    gate_full = [g[: device_count // 2].reshape(FF // 2, D) for g in gate_up_full]
    up_full = [g[device_count // 2 :].reshape(FF // 2, D) for g in gate_up_full]
    down_full = [down_all[:, h].reshape(FF // 2, D) for h in range(2)]
    qkv_full = first_full[:, :qkv_rows].reshape(-1, D)
    gain_parts = first_full[:, qkv_rows, :gain_len].reshape(-1)
    gain_in, gain_attn_post, gain_ffn_pre, gain_ffn_post, gain_query, gain_key = split_gains(
        gain_parts.astype(jnp.float32)
    )
    hidden = hidden_in.astype(jnp.float32)
    pos_group = positions[0]
    id_group = seg_ids[0]
    own_start = seq_place * row_count
    pos_own = lax.dynamic_slice_in_dim(pos_group, own_start, row_count)
    id_own = lax.dynamic_slice_in_dim(id_group, own_start, row_count)
    angles = turn_angles(pos_own)
    normed_in, inverse_in = norm_forward(hidden)
    attn_in = (normed_in * gain_in).astype(jnp.bfloat16)
    projected = jnp.einsum(
        "rd,cd->rc", attn_in, qkv_full, preferred_element_type=jnp.float32
    )
    query_raw = projected[:, : H * HD].reshape(row_count, H, HD)
    key_raw = projected[:, H * HD : (H + 1) * HD]
    value_low = projected[:, (H + 1) * HD :].astype(jnp.bfloat16)
    query_normed, query_inverse = norm_forward(query_raw)
    query_low = (rope_turn(query_normed * gain_query, angles[:, None, :]) * query_scale).astype(
        jnp.bfloat16
    )
    key_normed, key_inverse = norm_forward(key_raw)
    key_low = rope_turn(key_normed * gain_key, angles).astype(jnp.bfloat16)
    key_parts = []
    value_parts = []
    pos_parts = []
    id_parts = []
    live_parts = []
    back_step = 1
    got_pair = from_behind(jnp.concatenate([key_low, value_low], 1), "seq", back_step)
    got_key, got_value = got_pair[:, :HD], got_pair[:, HD:]
    source = seq_place - back_step
    source_start = jnp.maximum(source, 0) * row_count
    key_parts.append(got_key)
    value_parts.append(got_value)
    pos_parts.append(lax.dynamic_slice_in_dim(pos_group, source_start, row_count))
    id_parts.append(lax.dynamic_slice_in_dim(id_group, source_start, row_count))
    live_parts.append(jnp.broadcast_to(source >= 0, (row_count,)))
    key_parts.append(key_low)
    value_parts.append(value_low)
    pos_parts.append(pos_own)
    id_parts.append(id_own)
    live_parts.append(jnp.ones((row_count,), dtype=bool))
    keys_all = jnp.concatenate(key_parts, 0)
    values_all = jnp.concatenate(value_parts, 0)
    pos_keys = jnp.concatenate(pos_parts, 0)
    id_keys = jnp.concatenate(id_parts, 0)
    live_keys = jnp.concatenate(live_parts, 0)
    pos_gap = pos_own[:, None] - pos_keys[None, :]
    allowed = (
        live_keys[None, :]
        & (id_own[:, None] == id_keys[None, :])
        & (pos_gap >= 0)
        & (pos_gap < WINDOW)
    )
    scores = jnp.einsum("qhd,kd->hqk", query_low, keys_all, preferred_element_type=jnp.float32)
    scores = jnp.where(allowed[None], scores, MASKED_OUT)
    top_score = jnp.max(scores, -1, keepdims=True)
    weights_exp = jnp.exp(scores - top_score)
    weight_sum = jnp.sum(weights_exp, -1, keepdims=True)
    log_total = top_score + jnp.log(weight_sum)
    probs_low = (weights_exp / weight_sum).astype(jnp.bfloat16)
    attended = jnp.einsum("hqk,kd->qhd", probs_low, values_all, preferred_element_type=jnp.float32)
    attended = attended.reshape(row_count, H * HD).astype(jnp.bfloat16)
    branch = jnp.dot(attended, out_full, preferred_element_type=jnp.float32)
    branch_normed, branch_inverse = norm_forward(branch)
    middle = hidden + branch_normed * gain_attn_post
    ffn_normed, ffn_inverse = norm_forward(middle)
    ffn_in = (ffn_normed * gain_ffn_pre).astype(jnp.bfloat16)
    gate_halves, up_halves, mixed, pulls = [], [], [], []
    down_val = 0.0
    for half in range(2):
        gate_val = jnp.einsum(
            "rd,fd->rf", ffn_in, gate_full[half], preferred_element_type=jnp.float32
        )
        up_val = jnp.einsum("rd,fd->rf", ffn_in, up_full[half], preferred_element_type=jnp.float32)
        mixed_val, gelu_pull = jax.vjp(
            lambda gate_in, up_in: jax.nn.gelu(gate_in, approximate=True) * up_in, gate_val, up_val
        )
        pulls.append(gelu_pull)
        mixed.append(mixed_val.astype(jnp.bfloat16))
        down_val = down_val + jnp.dot(
            mixed[half], down_full[half], preferred_element_type=jnp.float32
        )
    down_normed, down_inverse = norm_forward(down_val)
    output = (middle + down_normed * gain_ffn_post).astype(jnp.bfloat16)
    grad_output = cotangent.astype(jnp.float32)
    grad_ffn_post = jnp.sum(grad_output * down_normed, 0)
    grad_down = norm_back(down_normed, down_inverse, grad_output * gain_ffn_post).astype(
        jnp.bfloat16
    )
    gate_up_shares, down_parts = [], []
    grad_ffn_in = 0.0
    for half, order in ((0, order_a), (1, order_b)):
        grad_mixed = jnp.einsum(
            "rd,fd->rf", grad_down, down_full[half], preferred_element_type=jnp.float32
        )
        down_parts.append(
            jnp.einsum("rf,rd->fd", mixed[half], grad_down, preferred_element_type=jnp.float32)
            .astype(jnp.bfloat16)
            .reshape(-1, 1, half_rows, D)
        )
        grad_gate, grad_up = pulls[half](grad_mixed)
        grad_gate = grad_gate.astype(jnp.bfloat16)
        grad_up = grad_up.astype(jnp.bfloat16)
        parts = [
            jnp.einsum("rf,rd->fd", part, ffn_in, preferred_element_type=jnp.float32)
            .astype(jnp.bfloat16)
            .reshape(-1, half_rows, D)
            for part in (grad_gate, grad_up)
        ]
        gate_up_shares.append(scatter_rows(jnp.concatenate(parts, 0), order, places))
        grad_ffn_in = grad_ffn_in + jnp.dot(
            grad_gate, gate_full[half], preferred_element_type=jnp.float32
        )
        grad_ffn_in = grad_ffn_in + jnp.dot(
            grad_up, up_full[half], preferred_element_type=jnp.float32
        )
    gate_up_share = jnp.concatenate(gate_up_shares, 0).T
    down_share = scatter_rows(
        jnp.concatenate(down_parts, 1).reshape(-1, half_rows, D), order_a, places
    )
    grad_ffn_pre = jnp.sum(grad_ffn_in * ffn_normed, 0)
    grad_middle = grad_output + norm_back(ffn_normed, ffn_inverse, grad_ffn_in * gain_ffn_pre)
    grad_attn_post = jnp.sum(grad_middle * branch_normed, 0)
    grad_branch = norm_back(branch_normed, branch_inverse, grad_middle * gain_attn_post).astype(
        jnp.bfloat16
    )
    grad_out_w = jnp.einsum("ra,rd->ad", attended, grad_branch, preferred_element_type=jnp.float32)
    grad_attended = jnp.einsum(
        "rd,ad->ra", grad_branch, out_full, preferred_element_type=jnp.float32
    )
    grad_attended = grad_attended.astype(jnp.bfloat16).reshape(row_count, H, HD)
    scores_again = jnp.einsum(
        "qhd,kd->hqk", query_low, keys_all, preferred_element_type=jnp.float32
    )
    scores_again = jnp.where(allowed[None], scores_again, MASKED_OUT)
    probs = jnp.exp(scores_again - log_total)
    probs_again = probs.astype(jnp.bfloat16)
    grad_probs = jnp.einsum(
        "qhd,kd->hqk", grad_attended, values_all, preferred_element_type=jnp.float32
    )
    grad_values = jnp.einsum(
        "hqk,qhd->kd", probs_again, grad_attended, preferred_element_type=jnp.float32
    )
    inner_sum = jnp.sum(probs * grad_probs, -1, keepdims=True)
    grad_scores = (probs * (grad_probs - inner_sum)).astype(jnp.bfloat16)
    grad_query = jnp.einsum(
        "hqk,kd->qhd", grad_scores, keys_all, preferred_element_type=jnp.float32
    )
    grad_keys = jnp.einsum(
        "hqk,qhd->kd", grad_scores, query_low, preferred_element_type=jnp.float32
    )
    own_first = reach_count * row_count
    grad_key_own = grad_keys[own_first:]
    grad_value_own = grad_values[own_first:]
    back_step = 1
    first_row = (reach_count - back_step) * row_count
    got_grad = from_behind(
        jnp.concatenate(
            [
                grad_keys[first_row : first_row + row_count],
                grad_values[first_row : first_row + row_count],
            ],
            1,
        ).astype(jnp.bfloat16),
        "seq",
        -back_step,
    ).astype(jnp.float32)
    got_grad_key, got_grad_value = got_grad[:, :HD], got_grad[:, HD:]
    grad_key_own = grad_key_own + got_grad_key
    grad_value_own = grad_value_own + got_grad_value
    grad_key_turn = rope_back(grad_key_own, angles)
    grad_key_gain = jnp.sum(grad_key_turn * key_normed, 0)
    grad_key_raw = norm_back(key_normed, key_inverse, grad_key_turn * gain_key).astype(jnp.bfloat16)
    grad_query_turn = rope_back(grad_query * query_scale, angles[:, None, :])
    grad_query_gain = jnp.sum(grad_query_turn * query_normed, (0, 1))
    grad_query_raw = norm_back(query_normed, query_inverse, grad_query_turn * gain_query)
    grad_query_raw = grad_query_raw.reshape(row_count, H * HD).astype(jnp.bfloat16)
    grad_projected = jnp.concatenate(
        [grad_query_raw, grad_key_raw, grad_value_own.astype(jnp.bfloat16)], 1
    )
    grad_qkv_w = jnp.einsum(
        "rc,rd->cd", grad_projected, attn_in, preferred_element_type=jnp.float32
    )
    grad_attn_in = jnp.einsum(
        "rc,cd->rd", grad_projected, qkv_full, preferred_element_type=jnp.float32
    )
    grad_in_gain = jnp.sum(grad_attn_in * normed_in, 0)
    input_grad = grad_middle + norm_back(normed_in, inverse_in, grad_attn_in * gain_in)
    grad_gains = jnp.concatenate(
        [grad_in_gain, grad_attn_post, grad_ffn_pre, grad_ffn_post, grad_query_gain, grad_key_gain]
    )
    qkv_share = scatter_rows(
        grad_qkv_w.astype(jnp.bfloat16).reshape(device_count, -1, D), order_a, places
    ).T
    out_share = scatter_rows(
        grad_out_w.astype(jnp.bfloat16).reshape(device_count, -1, D), order_b, places
    )
    gain_share = scatter_exact(grad_gains, order_b, places)
    return (output, input_grad, gain_share, qkv_share, out_share, gate_up_share, down_share)


def solution(mesh):
    in_specs = (
        P(("dp", "seq"), None),
        P(("dp", "seq"), None),
        P("dp", None),
        P("dp", None),
        P(("dp", "seq")),
        P(None, ("dp", "seq")),
        P(("dp", "seq"), None),
        P(None, ("dp", "seq")),
        P(("dp", "seq"), None),
    )
    out_specs = (
        P(("dp", "seq"), None),
        P(("dp", "seq"), None),
        P(("dp", "seq")),
        P(None, ("dp", "seq")),
        P(("dp", "seq"), None),
        P(None, ("dp", "seq")),
        P(("dp", "seq"), None),
    )
    return jax.shard_map(body, mesh=mesh, in_specs=in_specs, out_specs=out_specs, check_vma=False)
```

```python
import jax
import jax.numpy as jnp
from jax import lax
from jax.experimental import pallas as pl
from jax.experimental.pallas import tpu as pltpu
from jax.sharding import PartitionSpec as P

D = 640
H = 4
HD = 256
FF = 2048
WINDOW = 512


NORM_EPS = 1e-06
MASKED_OUT = -1e30


def from_behind(block, axis, distance):
    devices = range(lax.axis_size(axis))
    route = [(i - distance, i) for i in devices if i - distance in devices]
    return lax.ppermute(block, axis, route)


def norm_forward(values):
    inverse = lax.rsqrt(jnp.mean(values * values, -1, keepdims=True) + NORM_EPS)
    return (values * inverse, inverse)


def norm_back(normed, inverse, grad_normed):
    return inverse * (grad_normed - normed * jnp.mean(grad_normed * normed, -1, keepdims=True))


def turn_angles(pos_vals):
    half_dim = HD // 2
    inverse_freq = jnp.power(10000.0, -(2.0 * jnp.arange(half_dim, dtype=jnp.float32)) / HD)
    return pos_vals.astype(jnp.float32)[:, None] * inverse_freq[None, :]


def rope_turn(values, angles):
    half_dim = values.shape[-1] // 2
    first_half = values[..., :half_dim]
    second_half = values[..., half_dim:]
    cosine = jnp.cos(angles)
    sine_val = jnp.sin(angles)
    return jnp.concatenate(
        [
            first_half * cosine - second_half * sine_val,
            second_half * cosine + first_half * sine_val,
        ],
        -1,
    )


def rope_back(grads, angles):
    half_dim = grads.shape[-1] // 2
    first_half = grads[..., :half_dim]
    second_half = grads[..., half_dim:]
    cosine = jnp.cos(angles)
    sine_val = jnp.sin(angles)
    return jnp.concatenate(
        [
            first_half * cosine + second_half * sine_val,
            second_half * cosine - first_half * sine_val,
        ],
        -1,
    )


def split_gains(gain_vec):
    return (
        gain_vec[0:D],
        gain_vec[D : 2 * D],
        gain_vec[2 * D : 3 * D],
        gain_vec[3 * D : 4 * D],
        gain_vec[4 * D : 4 * D + HD],
        gain_vec[4 * D + HD : 4 * D + 2 * HD],
    )


def bit_orders():
    dp_bits = lax.axis_size("dp").bit_length() - 1
    seq_bits = lax.axis_size("seq").bit_length() - 1
    places = [("dp", b) for b in reversed(range(dp_bits))]
    places += [("seq", b) for b in reversed(range(seq_bits))]
    far = [("dp", b) for b in reversed(range(1, dp_bits))]
    low_dp = [("dp", 0)]
    high_seq = [("seq", b) for b in reversed(range(1, seq_bits))]
    last = [("seq", 0)]
    return places, far, low_dp + high_seq, high_seq + low_dp, last


def swap(block, axis, bit):
    route = [(i, i ^ (1 << bit)) for i in range(lax.axis_size(axis))]
    return lax.ppermute(block, axis, route)


def own_bit(axis, bit):
    return (lax.axis_index(axis) >> bit) & 1


def cut_rows(rows):
    tiles = rows // 16
    count = min(6, tiles)
    edges = [tiles * k // count * 16 for k in range(count + 1)]
    return [(edges[k], edges[k + 1] - edges[k]) for k in range(count)]


def gather_kernel(pack_ref, full_ref, local_sem, send_sem, recv_sem):
    far_size, _, high_size = full_ref.shape[:3]
    dp_at = lax.axis_index("dp")
    seq_at = lax.axis_index("seq")
    far, low = dp_at // 2, dp_at % 2
    high, core = seq_at // 2, seq_at % 2
    far_peers = [(((far + d) % far_size) * 2 + low, seq_at) for d in range(1, far_size)]
    low_peer = [(far * 2 + 1 - low, seq_at)]
    high_peers = [(dp_at, ((high + d) % high_size) * 2 + core) for d in range(1, high_size)]
    core_peer = [(dp_at, high * 2 + 1 - core)]
    groups = [far_peers, low_peer, high_peers, core_peer]
    slots = [0, far_size - 1, far_size, far_size + high_size - 1]
    barrier = pltpu.get_barrier_semaphore()
    peers = far_peers + low_peer + high_peers + core_peer
    for peer in peers:
        pl.semaphore_signal(barrier, inc=1, device_id=peer, device_id_type=pl.DeviceIdType.MESH)
    pl.semaphore_wait(barrier, len(peers))
    chunks = cut_rows(pack_ref.shape[0])
    every = slice(None)

    def copies(chunk, stage):
        start, size = chunks[chunk]
        rows = pl.ds(start, size)
        low_first = chunk % 2 == 0
        if stage == 0:
            kind, src, place = 0, pack_ref.at[rows], (far, low, high, core)
        elif stage == 3:
            kind, src, place = 3, None, (every, every, every, core)
        elif stage == 1:
            kind, src, place = (1 if low_first else 2), None, (every, low, high, core)
        elif low_first:
            kind, src, place = 2, None, (every, every, high, core)
        else:
            kind, src, place = 1, None, (every, low, every, core)
        target = full_ref.at[place + (rows,)]
        return [
            pltpu.make_async_remote_copy(
                src_ref=target if src is None else src,
                dst_ref=target,
                send_sem=send_sem.at[chunk, slots[kind] + k],
                recv_sem=recv_sem.at[chunk, slots[kind] + k],
                device_id=peer,
                device_id_type=pl.DeviceIdType.MESH,
            )
            for k, peer in enumerate(groups[kind])
        ]

    for chunk in range(len(chunks)):
        for copy in copies(chunk, 0):
            copy.start()
    own = pltpu.make_async_copy(pack_ref, full_ref.at[far, low, high, core], local_sem)
    own.start()
    own.wait()
    for turn in range((len(chunks) + 1) // 2 + 3):
        for stage in range(4):
            for chunk in (2 * (turn - stage), 2 * (turn - stage) + 1):
                if 0 <= chunk < len(chunks):
                    for copy in copies(chunk, stage):
                        copy.wait_recv()
                    if stage < 3:
                        for copy in copies(chunk, stage + 1):
                            copy.start()
    for chunk in range(len(chunks)):
        for stage in range(4):
            for copy in copies(chunk, stage):
                copy.wait_send()


def gather_rows(pack):
    far_size = lax.axis_size("dp") // 2
    high_size = lax.axis_size("seq") // 2
    chunk_count = len(cut_rows(pack.shape[0]))
    sem_count = far_size + high_size
    full = pl.pallas_call(
        gather_kernel,
        out_shape=jax.ShapeDtypeStruct((far_size, 2, high_size, 2) + pack.shape, pack.dtype),
        in_specs=[pl.BlockSpec(memory_space=pl.ANY)],
        out_specs=pl.BlockSpec(memory_space=pl.ANY),
        scratch_shapes=[
            pltpu.SemaphoreType.DMA,
            pltpu.SemaphoreType.DMA((chunk_count, sem_count)),
            pltpu.SemaphoreType.DMA((chunk_count, sem_count)),
        ],
        compiler_params=pltpu.CompilerParams(collective_id=0, has_side_effects=True),
    )(pack)
    return full.reshape((-1,) + pack.shape)


def pack_exact(values):
    high = lax.reduce_precision(values, 8, 7)
    row = jnp.concatenate([high, values - high], -1).astype(jnp.bfloat16)
    pads = [(0, 0)] * (row.ndim - 1) + [(0, 15), (0, D - row.shape[-1])]
    return jnp.pad(row[..., None, :], pads)


def unpack_exact(rows, length):
    row = rows[..., 0, : 2 * length].astype(jnp.float32)
    return row[..., :length] + row[..., length:]


def take_half(block, mine, at):
    return (
        lax.dynamic_index_in_dim(block, 1 - mine, at, keepdims=False),
        lax.dynamic_index_in_dim(block, mine, at, keepdims=False),
    )


def scatter_steps(block, exact, steps, left, places, final=False):
    left = list(left)
    for number, (axis, bit) in enumerate(reversed(steps)):
        at = left.index((axis, bit))
        mine = own_bit(axis, bit)
        give, keep = take_half(block, mine, at)
        rows = give.shape[-2]
        if exact is not None:
            exact_give, exact_keep = take_half(exact, mine, at)
            give = jnp.concatenate([give, pack_exact(exact_give)], -2)
        got = swap(give, axis, bit)
        block = keep.astype(jnp.float32) + got[..., :rows, :].astype(jnp.float32)
        if not (final and number == len(steps) - 1):
            block = block.astype(jnp.bfloat16)
        if exact is not None:
            exact = exact_keep + unpack_exact(got[..., rows:, :], exact.shape[-1])
        left.remove((axis, bit))
    return block, exact


def scatter_last(first, second, exact, plan):
    places, far, order_a, order_b, last = plan
    bits = (2,) * len(places)
    first = first.reshape(bits + first.shape[-2:])
    second = second.reshape(bits + second.shape[-2:])
    if exact is not None:
        exact = exact.reshape(bits + (-1,))
    first, _ = scatter_steps(first, None, last, places, places)
    second, exact = scatter_steps(second, exact, last, places, places)
    return first, second, exact


def scatter_near(first, second, exact, plan):
    places, far, order_a, order_b, last = plan
    left = far + [p for p in places if p not in far and p not in last]
    first, _ = scatter_steps(first, None, order_a, left, places)
    second, exact = scatter_steps(second, exact, order_b, left, places)
    return jnp.concatenate([first, second], -2), exact


def scatter_far(both, exact, plan):
    places, far, order_a, order_b, last = plan
    return scatter_steps(both, exact, far, far, places, final=True)


def body(hidden_in, cotangent, seg_ids, positions, norm_gains, w_qkv, w_out, w_gate_up, w_down):
    row_count = hidden_in.shape[0]
    seq_count = lax.axis_size("seq")
    seq_place = lax.axis_index("seq")
    reach_count = min(seq_count - 1, (WINDOW + row_count - 2) // row_count)
    query_scale = HD ** (-0.5)
    plan = bit_orders()
    device_count = lax.axis_size("dp") * seq_count
    gain_len = norm_gains.shape[0]
    qkv_rows = w_qkv.shape[1]
    out_rows = w_out.shape[0]
    gate_up_rows = w_gate_up.shape[1]
    gain_row = jnp.pad(norm_gains.reshape(1, gain_len), ((0, 0), (0, D - gain_len)))
    lead_rows = qkv_rows + out_rows
    lead_pad = -(lead_rows + 1) % 16
    ffn_start = lead_rows + 1 + lead_pad
    pack = jnp.concatenate(
        [
            w_qkv.T,
            w_out,
            jnp.pad(gain_row, ((0, lead_pad), (0, 0))),
            w_gate_up.T,
            w_down,
        ],
        0,
    )
    pack = jnp.pad(pack, ((0, -pack.shape[0] % 16), (0, 0)))
    full = gather_rows(pack)
    qkv_full = full[:, :qkv_rows].reshape(-1, D)
    out_full = full[:, qkv_rows:lead_rows].reshape(-1, D)
    gain_parts = full[:, lead_rows, :gain_len].reshape(-1)
    down_start = ffn_start + gate_up_rows
    gate_up_full = full[:, ffn_start:down_start].reshape(-1, D)
    down_full = full[:, down_start : down_start + w_down.shape[0]].reshape(-1, D)
    gain_in, gain_attn_post, gain_ffn_pre, gain_ffn_post, gain_query, gain_key = split_gains(
        gain_parts.astype(jnp.float32)
    )
    hidden = hidden_in.astype(jnp.float32)
    pos_group = positions[0]
    id_group = seg_ids[0]
    own_start = seq_place * row_count
    pos_own = lax.dynamic_slice_in_dim(pos_group, own_start, row_count)
    id_own = lax.dynamic_slice_in_dim(id_group, own_start, row_count)
    angles = turn_angles(pos_own)
    normed_in, inverse_in = norm_forward(hidden)
    attn_in = (normed_in * gain_in).astype(jnp.bfloat16)
    projected = jnp.einsum(
        "rd,cd->rc", attn_in, qkv_full, preferred_element_type=jnp.float32
    )
    query_raw = projected[:, : H * HD].reshape(row_count, H, HD)
    key_raw = projected[:, H * HD : (H + 1) * HD]
    value_low = projected[:, (H + 1) * HD :].astype(jnp.bfloat16)
    query_normed, query_inverse = norm_forward(query_raw)
    query_low = (rope_turn(query_normed * gain_query, angles[:, None, :]) * query_scale).astype(
        jnp.bfloat16
    )
    key_normed, key_inverse = norm_forward(key_raw)
    key_low = rope_turn(key_normed * gain_key, angles).astype(jnp.bfloat16)
    key_parts = []
    value_parts = []
    pos_parts = []
    id_parts = []
    live_parts = []
    back_step = 1
    got_pair = from_behind(jnp.concatenate([key_low, value_low], 1), "seq", back_step)
    got_key, got_value = got_pair[:, :HD], got_pair[:, HD:]
    source = seq_place - back_step
    source_start = jnp.maximum(source, 0) * row_count
    key_parts.append(got_key)
    value_parts.append(got_value)
    pos_parts.append(lax.dynamic_slice_in_dim(pos_group, source_start, row_count))
    id_parts.append(lax.dynamic_slice_in_dim(id_group, source_start, row_count))
    live_parts.append(jnp.broadcast_to(source >= 0, (row_count,)))
    key_parts.append(key_low)
    value_parts.append(value_low)
    pos_parts.append(pos_own)
    id_parts.append(id_own)
    live_parts.append(jnp.ones((row_count,), dtype=bool))
    keys_all = jnp.concatenate(key_parts, 0)
    values_all = jnp.concatenate(value_parts, 0)
    pos_keys = jnp.concatenate(pos_parts, 0)
    id_keys = jnp.concatenate(id_parts, 0)
    live_keys = jnp.concatenate(live_parts, 0)
    pos_gap = pos_own[:, None] - pos_keys[None, :]
    allowed = (
        live_keys[None, :]
        & (id_own[:, None] == id_keys[None, :])
        & (pos_gap >= 0)
        & (pos_gap < WINDOW)
    )
    scores = jnp.einsum("qhd,kd->hqk", query_low, keys_all, preferred_element_type=jnp.float32)
    scores = jnp.where(allowed[None], scores, MASKED_OUT)
    top_score = jnp.max(scores, -1, keepdims=True)
    weights_exp = jnp.exp(scores - top_score)
    weight_sum = jnp.sum(weights_exp, -1, keepdims=True)
    log_total = top_score + jnp.log(weight_sum)
    probs_low = (weights_exp / weight_sum).astype(jnp.bfloat16)
    attended = jnp.einsum("hqk,kd->qhd", probs_low, values_all, preferred_element_type=jnp.float32)
    attended = attended.reshape(row_count, H * HD).astype(jnp.bfloat16)
    branch = jnp.dot(attended, out_full, preferred_element_type=jnp.float32)
    branch_normed, branch_inverse = norm_forward(branch)
    middle = hidden + branch_normed * gain_attn_post
    ffn_normed, ffn_inverse = norm_forward(middle)
    ffn_in = (ffn_normed * gain_ffn_pre).astype(jnp.bfloat16)
    gate_up = jnp.einsum("rd,fd->rf", ffn_in, gate_up_full, preferred_element_type=jnp.float32)
    mixed_val, gelu_pull = jax.vjp(
        lambda gate_in, up_in: jax.nn.gelu(gate_in, approximate=True) * up_in,
        gate_up[:, :FF],
        gate_up[:, FF:],
    )
    mixed = mixed_val.astype(jnp.bfloat16)
    down_val = jnp.dot(mixed, down_full, preferred_element_type=jnp.float32)
    down_normed, down_inverse = norm_forward(down_val)
    output = (middle + down_normed * gain_ffn_post).astype(jnp.bfloat16)
    grad_output = cotangent.astype(jnp.float32)
    grad_ffn_post = jnp.sum(grad_output * down_normed, 0)
    grad_down = norm_back(down_normed, down_inverse, grad_output * gain_ffn_post).astype(
        jnp.bfloat16
    )
    grad_mixed = jnp.einsum("rd,fd->rf", grad_down, down_full, preferred_element_type=jnp.float32)
    grad_down_w = jnp.einsum("rf,rd->fd", mixed, grad_down, preferred_element_type=jnp.float32)
    grad_down_w = grad_down_w.astype(jnp.bfloat16).reshape(device_count, -1, D)
    grad_gate, grad_up = gelu_pull(grad_mixed)
    grad_gate_up = jnp.concatenate([grad_gate, grad_up], 1).astype(jnp.bfloat16)
    grad_gate_up_w = jnp.einsum(
        "rf,rd->fd", grad_gate_up, ffn_in, preferred_element_type=jnp.float32
    )
    grad_gate_up_w = grad_gate_up_w.astype(jnp.bfloat16).reshape(device_count, -1, D)
    grad_ffn_in = jnp.dot(grad_gate_up, gate_up_full, preferred_element_type=jnp.float32)
    grad_down_w, grad_gate_up_w, grad_ffn_in = lax.optimization_barrier(
        (grad_down_w, grad_gate_up_w, grad_ffn_in)
    )
    cut = (grad_down_w.shape[1] + gate_up_rows) // 2
    ffn_a, ffn_b, _ = scatter_last(
        grad_gate_up_w[:, :cut],
        jnp.concatenate([grad_gate_up_w[:, cut:], grad_down_w], 1),
        None,
        plan,
    )
    grad_ffn_pre = jnp.sum(grad_ffn_in * ffn_normed, 0)
    grad_middle = grad_output + norm_back(ffn_normed, ffn_inverse, grad_ffn_in * gain_ffn_pre)
    grad_attn_post = jnp.sum(grad_middle * branch_normed, 0)
    grad_branch = norm_back(branch_normed, branch_inverse, grad_middle * gain_attn_post).astype(
        jnp.bfloat16
    )
    grad_out_w = jnp.einsum("ra,rd->ad", attended, grad_branch, preferred_element_type=jnp.float32)
    grad_attended = jnp.einsum(
        "rd,ad->ra", grad_branch, out_full, preferred_element_type=jnp.float32
    )
    grad_attended = grad_attended.astype(jnp.bfloat16).reshape(row_count, H, HD)
    scores_again = jnp.einsum(
        "qhd,kd->hqk", query_low, keys_all, preferred_element_type=jnp.float32
    )
    scores_again = jnp.where(allowed[None], scores_again, MASKED_OUT)
    probs = jnp.exp(scores_again - log_total)
    probs_again = probs.astype(jnp.bfloat16)
    grad_probs = jnp.einsum(
        "qhd,kd->hqk", grad_attended, values_all, preferred_element_type=jnp.float32
    )
    grad_values = jnp.einsum(
        "hqk,qhd->kd", probs_again, grad_attended, preferred_element_type=jnp.float32
    )
    inner_sum = jnp.sum(probs * grad_probs, -1, keepdims=True)
    grad_scores = (probs * (grad_probs - inner_sum)).astype(jnp.bfloat16)
    grad_scores, ffn_a, ffn_b = lax.optimization_barrier((grad_scores, ffn_a, ffn_b))
    ffn_near, _ = scatter_near(ffn_a, ffn_b, None, plan)
    grad_query = jnp.einsum(
        "hqk,kd->qhd", grad_scores, keys_all, preferred_element_type=jnp.float32
    )
    grad_keys = jnp.einsum(
        "hqk,qhd->kd", grad_scores, query_low, preferred_element_type=jnp.float32
    )
    grad_query, grad_keys, ffn_near = lax.optimization_barrier((grad_query, grad_keys, ffn_near))
    ffn_share, _ = scatter_far(ffn_near, None, plan)
    own_first = reach_count * row_count
    grad_key_own = grad_keys[own_first:]
    grad_value_own = grad_values[own_first:]
    back_step = 1
    first_row = (reach_count - back_step) * row_count
    got_grad = from_behind(
        jnp.concatenate(
            [
                grad_keys[first_row : first_row + row_count],
                grad_values[first_row : first_row + row_count],
            ],
            1,
        ).astype(jnp.bfloat16),
        "seq",
        -back_step,
    ).astype(jnp.float32)
    got_grad_key, got_grad_value = got_grad[:, :HD], got_grad[:, HD:]
    grad_key_own = grad_key_own + got_grad_key
    grad_value_own = grad_value_own + got_grad_value
    grad_key_turn = rope_back(grad_key_own, angles)
    grad_key_gain = jnp.sum(grad_key_turn * key_normed, 0)
    grad_key_raw = norm_back(key_normed, key_inverse, grad_key_turn * gain_key).astype(jnp.bfloat16)
    grad_query_turn = rope_back(grad_query * query_scale, angles[:, None, :])
    grad_query_gain = jnp.sum(grad_query_turn * query_normed, (0, 1))
    grad_query_raw = norm_back(query_normed, query_inverse, grad_query_turn * gain_query)
    grad_query_raw = grad_query_raw.reshape(row_count, H * HD).astype(jnp.bfloat16)
    grad_projected = jnp.concatenate(
        [grad_query_raw, grad_key_raw, grad_value_own.astype(jnp.bfloat16)], 1
    )
    grad_projected, ffn_share = (grad_projected, ffn_share)
    gate_up_share = ffn_share[:gate_up_rows].T
    down_share = ffn_share[gate_up_rows:]
    grad_qkv_w = jnp.einsum(
        "rc,rd->cd", grad_projected, attn_in, preferred_element_type=jnp.float32
    )
    grad_attn_in = jnp.einsum(
        "rc,cd->rd", grad_projected, qkv_full, preferred_element_type=jnp.float32
    )
    grad_in_gain = jnp.sum(grad_attn_in * normed_in, 0)
    input_grad = grad_middle + norm_back(normed_in, inverse_in, grad_attn_in * gain_in)
    grad_gains = jnp.concatenate(
        [grad_in_gain, grad_attn_post, grad_ffn_pre, grad_ffn_post, grad_query_gain, grad_key_gain]
    )
    parts = scatter_last(
        grad_qkv_w.astype(jnp.bfloat16).reshape(device_count, -1, D),
        grad_out_w.astype(jnp.bfloat16).reshape(device_count, -1, D),
        grad_gains,
        plan,
    )
    first_share, gain_share = scatter_far(*scatter_near(*parts, plan), plan)
    qkv_share = first_share[:qkv_rows].T
    out_share = first_share[qkv_rows:]
    return (output, input_grad, gain_share, qkv_share, out_share, gate_up_share, down_share)


def solution(mesh):
    in_specs = (
        P(("dp", "seq"), None),
        P(("dp", "seq"), None),
        P("dp", None),
        P("dp", None),
        P(("dp", "seq")),
        P(None, ("dp", "seq")),
        P(("dp", "seq"), None),
        P(None, ("dp", "seq")),
        P(("dp", "seq"), None),
    )
    out_specs = (
        P(("dp", "seq"), None),
        P(("dp", "seq"), None),
        P(("dp", "seq")),
        P(None, ("dp", "seq")),
        P(("dp", "seq"), None),
        P(None, ("dp", "seq")),
        P(("dp", "seq"), None),
    )
    return jax.shard_map(body, mesh=mesh, in_specs=in_specs, out_specs=out_specs, check_vma=False)
```

```python
import functools

import jax
import jax.numpy as jnp
from jax import lax
from jax.experimental import pallas as pl
from jax.experimental.pallas import tpu as pltpu
from jax.sharding import PartitionSpec as P

D = 640
H = 4
HD = 256
FF = 2048
WINDOW = 512


NORM_EPS = 1e-06
MASKED_OUT = -1e30


def from_behind(block, axis, distance):
    devices = range(lax.axis_size(axis))
    route = [(i - distance, i) for i in devices if i - distance in devices]
    return lax.ppermute(block, axis, route)


def norm_forward(values):
    inverse = lax.rsqrt(jnp.mean(values * values, -1, keepdims=True) + NORM_EPS)
    return (values * inverse, inverse)


def norm_back(normed, inverse, grad_normed):
    return inverse * (grad_normed - normed * jnp.mean(grad_normed * normed, -1, keepdims=True))


def turn_angles(pos_vals):
    half_dim = HD // 2
    inverse_freq = jnp.power(10000.0, -(2.0 * jnp.arange(half_dim, dtype=jnp.float32)) / HD)
    return pos_vals.astype(jnp.float32)[:, None] * inverse_freq[None, :]


def rope_turn(values, angles):
    half_dim = values.shape[-1] // 2
    first_half = values[..., :half_dim]
    second_half = values[..., half_dim:]
    cosine = jnp.cos(angles)
    sine_val = jnp.sin(angles)
    return jnp.concatenate(
        [
            first_half * cosine - second_half * sine_val,
            second_half * cosine + first_half * sine_val,
        ],
        -1,
    )


def rope_back(grads, angles):
    half_dim = grads.shape[-1] // 2
    first_half = grads[..., :half_dim]
    second_half = grads[..., half_dim:]
    cosine = jnp.cos(angles)
    sine_val = jnp.sin(angles)
    return jnp.concatenate(
        [
            first_half * cosine + second_half * sine_val,
            second_half * cosine - first_half * sine_val,
        ],
        -1,
    )


def split_gains(gain_vec):
    return (
        gain_vec[0:D],
        gain_vec[D : 2 * D],
        gain_vec[2 * D : 3 * D],
        gain_vec[3 * D : 4 * D],
        gain_vec[4 * D : 4 * D + HD],
        gain_vec[4 * D + HD : 4 * D + 2 * HD],
    )


def bit_orders():
    dp_bits = lax.axis_size("dp").bit_length() - 1
    seq_bits = lax.axis_size("seq").bit_length() - 1
    places = [("dp", b) for b in reversed(range(dp_bits))]
    places += [("seq", b) for b in reversed(range(seq_bits))]
    far = [("dp", b) for b in reversed(range(1, dp_bits))]
    low_dp = [("dp", 0)]
    high_seq = [("seq", b) for b in reversed(range(1, seq_bits))]
    last = [("seq", 0)]
    return places, far, low_dp + high_seq, high_seq + low_dp, last


def swap(block, axis, bit):
    route = [(i, i ^ (1 << bit)) for i in range(lax.axis_size(axis))]
    return lax.ppermute(block, axis, route)


def own_bit(axis, bit):
    return (lax.axis_index(axis) >> bit) & 1


def cut_rows(row_counts):
    chunks = []
    for k, rows in enumerate(row_counts):
        parts = 2 if rows % 32 == 0 and rows >= 64 else 1
        chunks += [(k, p * rows // parts, rows // parts) for p in range(parts)]
    return chunks


def gather_kernel(count, *refs):
    pack_refs, full_refs = refs[:count], refs[count : 2 * count]
    local_sem, send_sem, recv_sem = refs[2 * count :]
    far_size, _, high_size = full_refs[0].shape[:3]
    dp_at = lax.axis_index("dp")
    seq_at = lax.axis_index("seq")
    far, low = dp_at // 2, dp_at % 2
    high, core = seq_at // 2, seq_at % 2
    far_peers = [(((far + d) % far_size) * 2 + low, seq_at) for d in range(1, far_size)]
    low_peer = [(far * 2 + 1 - low, seq_at)]
    high_peers = [(dp_at, ((high + d) % high_size) * 2 + core) for d in range(1, high_size)]
    core_peer = [(dp_at, high * 2 + 1 - core)]
    groups = [far_peers, low_peer, high_peers, core_peer]
    slots = [0, far_size - 1, far_size, far_size + high_size - 1]
    barrier = pltpu.get_barrier_semaphore()
    peers = far_peers + low_peer + high_peers + core_peer
    for peer in peers:
        pl.semaphore_signal(barrier, inc=1, device_id=peer, device_id_type=pl.DeviceIdType.MESH)
    pl.semaphore_wait(barrier, len(peers))
    chunks = cut_rows([ref.shape[0] for ref in pack_refs])
    every = slice(None)

    def copies(chunk, stage):
        which, start, size = chunks[chunk]
        rows = pl.ds(start, size)
        low_first = chunk % 2 == 0
        if stage == 0:
            kind, src, place = 0, pack_refs[which].at[rows], (far, low, high, core)
        elif stage == 3:
            kind, src, place = 3, None, (every, every, every, core)
        elif stage == 1:
            kind, src, place = (1 if low_first else 2), None, (every, low, high, core)
        elif low_first:
            kind, src, place = 2, None, (every, every, high, core)
        else:
            kind, src, place = 1, None, (every, low, every, core)
        target = full_refs[which].at[place + (rows,)]
        return [
            pltpu.make_async_remote_copy(
                src_ref=target if src is None else src,
                dst_ref=target,
                send_sem=send_sem.at[chunk, slots[kind] + k],
                recv_sem=recv_sem.at[chunk, slots[kind] + k],
                device_id=peer,
                device_id_type=pl.DeviceIdType.MESH,
            )
            for k, peer in enumerate(groups[kind])
        ]

    def launch(pair):
        for chunk in (2 * pair, 2 * pair + 1):
            if chunk < len(chunks):
                for copy in copies(chunk, 0):
                    copy.start()

    launch(0)
    own = [
        pltpu.make_async_copy(pack_refs[k], full_refs[k].at[far, low, high, core], local_sem.at[k])
        for k in range(count)
    ]
    for copy in own:
        copy.start()
    for copy in own:
        copy.wait()
    for turn in range((len(chunks) + 1) // 2 + 3):
        for stage in range(4):
            for chunk in (2 * (turn - stage), 2 * (turn - stage) + 1):
                if 0 <= chunk < len(chunks):
                    for copy in copies(chunk, stage):
                        copy.wait_recv()
                    if stage < 3:
                        for copy in copies(chunk, stage + 1):
                            copy.start()
                if stage == 0 and chunk % 2 == 1:
                    launch(turn + 1)
    for chunk in range(len(chunks)):
        for stage in range(4):
            for copy in copies(chunk, stage):
                copy.wait_send()


def gather_rows(packs):
    far_size = lax.axis_size("dp") // 2
    high_size = lax.axis_size("seq") // 2
    packs = [jnp.pad(pack, ((0, -pack.shape[0] % 16), (0, 0))) for pack in packs]
    chunk_count = len(cut_rows([pack.shape[0] for pack in packs]))
    sem_count = far_size + high_size
    fulls = pl.pallas_call(
        functools.partial(gather_kernel, len(packs)),
        out_shape=[
            jax.ShapeDtypeStruct((far_size, 2, high_size, 2) + pack.shape, pack.dtype)
            for pack in packs
        ],
        in_specs=[pl.BlockSpec(memory_space=pl.ANY)] * len(packs),
        out_specs=[pl.BlockSpec(memory_space=pl.ANY)] * len(packs),
        scratch_shapes=[
            pltpu.SemaphoreType.DMA((len(packs),)),
            pltpu.SemaphoreType.DMA((chunk_count, sem_count)),
            pltpu.SemaphoreType.DMA((chunk_count, sem_count)),
        ],
        compiler_params=pltpu.CompilerParams(collective_id=0, has_side_effects=True),
    )(*packs)
    return [full.reshape((-1,) + pack.shape) for full, pack in zip(fulls, packs)]


def pack_exact(values):
    high = lax.reduce_precision(values, 8, 7)
    row = jnp.concatenate([high, values - high], -1).astype(jnp.bfloat16)
    pads = [(0, 0)] * (row.ndim - 1) + [(0, 15), (0, D - row.shape[-1])]
    return jnp.pad(row[..., None, :], pads)


def unpack_exact(rows, length):
    row = rows[..., 0, : 2 * length].astype(jnp.float32)
    return row[..., :length] + row[..., length:]


def take_half(block, mine, at):
    return (
        lax.dynamic_index_in_dim(block, 1 - mine, at, keepdims=False),
        lax.dynamic_index_in_dim(block, mine, at, keepdims=False),
    )


def scatter_steps(block, exact, steps, left, places, final=False):
    left = list(left)
    for number, (axis, bit) in enumerate(reversed(steps)):
        at = left.index((axis, bit))
        mine = own_bit(axis, bit)
        give, keep = take_half(block, mine, at)
        rows = give.shape[-2]
        if exact is not None:
            exact_give, exact_keep = take_half(exact, mine, at)
            give = jnp.concatenate([give, pack_exact(exact_give)], -2)
        got = swap(give, axis, bit)
        block = keep.astype(jnp.float32) + got[..., :rows, :].astype(jnp.float32)
        if not (final and number == len(steps) - 1):
            block = block.astype(jnp.bfloat16)
        if exact is not None:
            exact = exact_keep + unpack_exact(got[..., rows:, :], exact.shape[-1])
        left.remove((axis, bit))
    return block, exact


def scatter_last(first, second, exact, plan):
    places, far, order_a, order_b, last = plan
    bits = (2,) * len(places)
    first = first.reshape(bits + first.shape[-2:])
    second = second.reshape(bits + second.shape[-2:])
    if exact is not None:
        exact = exact.reshape(bits + (-1,))
    first, _ = scatter_steps(first, None, last, places, places)
    second, exact = scatter_steps(second, exact, last, places, places)
    return first, second, exact


def scatter_near(first, second, exact, plan):
    places, far, order_a, order_b, last = plan
    left = far + [p for p in places if p not in far and p not in last]
    first, _ = scatter_steps(first, None, order_a, left, places)
    second, exact = scatter_steps(second, exact, order_b, left, places)
    return jnp.concatenate([first, second], -2), exact


def scatter_far(both, exact, plan):
    places, far, order_a, order_b, last = plan
    return scatter_steps(both, exact, far, far, places, final=True)


def body(hidden_in, cotangent, seg_ids, positions, norm_gains, w_qkv, w_out, w_gate_up, w_down):
    row_count = hidden_in.shape[0]
    seq_count = lax.axis_size("seq")
    seq_place = lax.axis_index("seq")
    reach_count = min(seq_count - 1, (WINDOW + row_count - 2) // row_count)
    query_scale = HD ** (-0.5)
    plan = bit_orders()
    device_count = lax.axis_size("dp") * seq_count
    gain_len = norm_gains.shape[0]
    qkv_rows = w_qkv.shape[1]
    out_rows = w_out.shape[0]
    gate_up_rows = w_gate_up.shape[1]
    gain_row = jnp.pad(norm_gains.reshape(1, gain_len), ((0, 0), (0, D - gain_len)))
    qkv_full, out_full, gate_up_full, down_full, gain_full = gather_rows(
        [w_qkv.T, w_out, w_gate_up.T, w_down, gain_row]
    )
    qkv_full = qkv_full[:, :qkv_rows].reshape(-1, D)
    out_full = out_full[:, :out_rows].reshape(-1, D)
    gate_up_full = gate_up_full[:, :gate_up_rows].reshape(-1, D)
    down_full = down_full[:, : w_down.shape[0]].reshape(-1, D)
    gain_parts = gain_full[:, 0, :gain_len].reshape(-1)
    gain_in, gain_attn_post, gain_ffn_pre, gain_ffn_post, gain_query, gain_key = split_gains(
        gain_parts.astype(jnp.float32)
    )
    hidden = hidden_in.astype(jnp.float32)
    pos_group = positions[0]
    id_group = seg_ids[0]
    own_start = seq_place * row_count
    pos_own = lax.dynamic_slice_in_dim(pos_group, own_start, row_count)
    id_own = lax.dynamic_slice_in_dim(id_group, own_start, row_count)
    angles = turn_angles(pos_own)
    normed_in, inverse_in = norm_forward(hidden)
    attn_in = (normed_in * gain_in).astype(jnp.bfloat16)
    projected = jnp.einsum(
        "rd,cd->rc", attn_in, qkv_full, preferred_element_type=jnp.float32
    )
    query_raw = projected[:, : H * HD].reshape(row_count, H, HD)
    key_raw = projected[:, H * HD : (H + 1) * HD]
    value_low = projected[:, (H + 1) * HD :].astype(jnp.bfloat16)
    query_normed, query_inverse = norm_forward(query_raw)
    query_low = (rope_turn(query_normed * gain_query, angles[:, None, :]) * query_scale).astype(
        jnp.bfloat16
    )
    key_normed, key_inverse = norm_forward(key_raw)
    key_low = rope_turn(key_normed * gain_key, angles).astype(jnp.bfloat16)
    key_parts = []
    value_parts = []
    pos_parts = []
    id_parts = []
    live_parts = []
    back_step = 1
    got_pair = from_behind(jnp.concatenate([key_low, value_low], 1), "seq", back_step)
    got_key, got_value = got_pair[:, :HD], got_pair[:, HD:]
    source = seq_place - back_step
    source_start = jnp.maximum(source, 0) * row_count
    key_parts.append(got_key)
    value_parts.append(got_value)
    pos_parts.append(lax.dynamic_slice_in_dim(pos_group, source_start, row_count))
    id_parts.append(lax.dynamic_slice_in_dim(id_group, source_start, row_count))
    live_parts.append(jnp.broadcast_to(source >= 0, (row_count,)))
    key_parts.append(key_low)
    value_parts.append(value_low)
    pos_parts.append(pos_own)
    id_parts.append(id_own)
    live_parts.append(jnp.ones((row_count,), dtype=bool))
    keys_all = jnp.concatenate(key_parts, 0)
    values_all = jnp.concatenate(value_parts, 0)
    pos_keys = jnp.concatenate(pos_parts, 0)
    id_keys = jnp.concatenate(id_parts, 0)
    live_keys = jnp.concatenate(live_parts, 0)
    pos_gap = pos_own[:, None] - pos_keys[None, :]
    allowed = (
        live_keys[None, :]
        & (id_own[:, None] == id_keys[None, :])
        & (pos_gap >= 0)
        & (pos_gap < WINDOW)
    )
    scores = jnp.einsum("qhd,kd->hqk", query_low, keys_all, preferred_element_type=jnp.float32)
    scores = jnp.where(allowed[None], scores, MASKED_OUT)
    top_score = jnp.max(scores, -1, keepdims=True)
    weights_exp = jnp.exp(scores - top_score)
    weight_sum = jnp.sum(weights_exp, -1, keepdims=True)
    log_total = top_score + jnp.log(weight_sum)
    probs_low = (weights_exp / weight_sum).astype(jnp.bfloat16)
    attended = jnp.einsum("hqk,kd->qhd", probs_low, values_all, preferred_element_type=jnp.float32)
    attended = attended.reshape(row_count, H * HD).astype(jnp.bfloat16)
    branch = jnp.dot(attended, out_full, preferred_element_type=jnp.float32)
    branch_normed, branch_inverse = norm_forward(branch)
    middle = hidden + branch_normed * gain_attn_post
    ffn_normed, ffn_inverse = norm_forward(middle)
    ffn_in = (ffn_normed * gain_ffn_pre).astype(jnp.bfloat16)
    gate_up = jnp.einsum("rd,fd->rf", ffn_in, gate_up_full, preferred_element_type=jnp.float32)
    mixed_val, gelu_pull = jax.vjp(
        lambda gate_in, up_in: jax.nn.gelu(gate_in, approximate=True) * up_in,
        gate_up[:, :FF],
        gate_up[:, FF:],
    )
    mixed = mixed_val.astype(jnp.bfloat16)
    down_val = jnp.dot(mixed, down_full, preferred_element_type=jnp.float32)
    down_normed, down_inverse = norm_forward(down_val)
    output = (middle + down_normed * gain_ffn_post).astype(jnp.bfloat16)
    grad_output = cotangent.astype(jnp.float32)
    grad_ffn_post = jnp.sum(grad_output * down_normed, 0)
    grad_down = norm_back(down_normed, down_inverse, grad_output * gain_ffn_post).astype(
        jnp.bfloat16
    )
    grad_mixed = jnp.einsum("rd,fd->rf", grad_down, down_full, preferred_element_type=jnp.float32)
    grad_down_w = jnp.einsum("rf,rd->fd", mixed, grad_down, preferred_element_type=jnp.float32)
    grad_down_w = grad_down_w.astype(jnp.bfloat16).reshape(device_count, -1, D)
    grad_gate, grad_up = gelu_pull(grad_mixed)
    grad_gate_up = jnp.concatenate([grad_gate, grad_up], 1).astype(jnp.bfloat16)
    grad_gate_up_w = jnp.einsum(
        "rf,rd->fd", grad_gate_up, ffn_in, preferred_element_type=jnp.float32
    )
    grad_gate_up_w = grad_gate_up_w.astype(jnp.bfloat16).reshape(device_count, -1, D)
    grad_ffn_in = jnp.dot(grad_gate_up, gate_up_full, preferred_element_type=jnp.float32)
    grad_down_w, grad_gate_up_w, grad_ffn_in = lax.optimization_barrier(
        (grad_down_w, grad_gate_up_w, grad_ffn_in)
    )
    cut = (grad_down_w.shape[1] + gate_up_rows) // 2
    ffn_a, ffn_b, _ = scatter_last(
        grad_gate_up_w[:, :cut],
        jnp.concatenate([grad_gate_up_w[:, cut:], grad_down_w], 1),
        None,
        plan,
    )
    grad_ffn_pre = jnp.sum(grad_ffn_in * ffn_normed, 0)
    grad_middle = grad_output + norm_back(ffn_normed, ffn_inverse, grad_ffn_in * gain_ffn_pre)
    grad_attn_post = jnp.sum(grad_middle * branch_normed, 0)
    grad_branch = norm_back(branch_normed, branch_inverse, grad_middle * gain_attn_post).astype(
        jnp.bfloat16
    )
    grad_out_w = jnp.einsum("ra,rd->ad", attended, grad_branch, preferred_element_type=jnp.float32)
    grad_attended = jnp.einsum(
        "rd,ad->ra", grad_branch, out_full, preferred_element_type=jnp.float32
    )
    grad_attended = grad_attended.astype(jnp.bfloat16).reshape(row_count, H, HD)
    scores_again = jnp.einsum(
        "qhd,kd->hqk", query_low, keys_all, preferred_element_type=jnp.float32
    )
    scores_again = jnp.where(allowed[None], scores_again, MASKED_OUT)
    probs = jnp.exp(scores_again - log_total)
    probs_again = probs.astype(jnp.bfloat16)
    grad_probs = jnp.einsum(
        "qhd,kd->hqk", grad_attended, values_all, preferred_element_type=jnp.float32
    )
    grad_values = jnp.einsum(
        "hqk,qhd->kd", probs_again, grad_attended, preferred_element_type=jnp.float32
    )
    inner_sum = jnp.sum(probs * grad_probs, -1, keepdims=True)
    grad_scores = (probs * (grad_probs - inner_sum)).astype(jnp.bfloat16)
    grad_scores, ffn_a, ffn_b = lax.optimization_barrier((grad_scores, ffn_a, ffn_b))
    ffn_near, _ = scatter_near(ffn_a, ffn_b, None, plan)
    grad_query = jnp.einsum(
        "hqk,kd->qhd", grad_scores, keys_all, preferred_element_type=jnp.float32
    )
    grad_keys = jnp.einsum(
        "hqk,qhd->kd", grad_scores, query_low, preferred_element_type=jnp.float32
    )
    grad_query, grad_keys, ffn_near = lax.optimization_barrier((grad_query, grad_keys, ffn_near))
    ffn_share, _ = scatter_far(ffn_near, None, plan)
    own_first = reach_count * row_count
    grad_key_own = grad_keys[own_first:]
    grad_value_own = grad_values[own_first:]
    back_step = 1
    first_row = (reach_count - back_step) * row_count
    got_grad = from_behind(
        jnp.concatenate(
            [
                grad_keys[first_row : first_row + row_count],
                grad_values[first_row : first_row + row_count],
            ],
            1,
        ).astype(jnp.bfloat16),
        "seq",
        -back_step,
    ).astype(jnp.float32)
    got_grad_key, got_grad_value = got_grad[:, :HD], got_grad[:, HD:]
    grad_key_own = grad_key_own + got_grad_key
    grad_value_own = grad_value_own + got_grad_value
    grad_key_turn = rope_back(grad_key_own, angles)
    grad_key_gain = jnp.sum(grad_key_turn * key_normed, 0)
    grad_key_raw = norm_back(key_normed, key_inverse, grad_key_turn * gain_key).astype(jnp.bfloat16)
    grad_query_turn = rope_back(grad_query * query_scale, angles[:, None, :])
    grad_query_gain = jnp.sum(grad_query_turn * query_normed, (0, 1))
    grad_query_raw = norm_back(query_normed, query_inverse, grad_query_turn * gain_query)
    grad_query_raw = grad_query_raw.reshape(row_count, H * HD).astype(jnp.bfloat16)
    grad_projected = jnp.concatenate(
        [grad_query_raw, grad_key_raw, grad_value_own.astype(jnp.bfloat16)], 1
    )
    grad_projected, ffn_share = (grad_projected, ffn_share)
    gate_up_share = ffn_share[:gate_up_rows].T
    down_share = ffn_share[gate_up_rows:]
    grad_qkv_w = jnp.einsum(
        "rc,rd->cd", grad_projected, attn_in, preferred_element_type=jnp.float32
    )
    grad_attn_in = jnp.einsum(
        "rc,cd->rd", grad_projected, qkv_full, preferred_element_type=jnp.float32
    )
    grad_in_gain = jnp.sum(grad_attn_in * normed_in, 0)
    input_grad = grad_middle + norm_back(normed_in, inverse_in, grad_attn_in * gain_in)
    grad_gains = jnp.concatenate(
        [grad_in_gain, grad_attn_post, grad_ffn_pre, grad_ffn_post, grad_query_gain, grad_key_gain]
    )
    parts = scatter_last(
        grad_qkv_w.astype(jnp.bfloat16).reshape(device_count, -1, D),
        grad_out_w.astype(jnp.bfloat16).reshape(device_count, -1, D),
        grad_gains,
        plan,
    )
    first_share, gain_share = scatter_far(*scatter_near(*parts, plan), plan)
    qkv_share = first_share[:qkv_rows].T
    out_share = first_share[qkv_rows:]
    return (output, input_grad, gain_share, qkv_share, out_share, gate_up_share, down_share)


def solution(mesh):
    in_specs = (
        P(("dp", "seq"), None),
        P(("dp", "seq"), None),
        P("dp", None),
        P("dp", None),
        P(("dp", "seq")),
        P(None, ("dp", "seq")),
        P(("dp", "seq"), None),
        P(None, ("dp", "seq")),
        P(("dp", "seq"), None),
    )
    out_specs = (
        P(("dp", "seq"), None),
        P(("dp", "seq"), None),
        P(("dp", "seq")),
        P(None, ("dp", "seq")),
        P(("dp", "seq"), None),
        P(None, ("dp", "seq")),
        P(("dp", "seq"), None),
    )
    return jax.shard_map(body, mesh=mesh, in_specs=in_specs, out_specs=out_specs, check_vma=False)
```
